512 devices in a mesh: dp: 2 (over x_hi), ctx: 32 (over x_lo, y, core), head: 8 (over z).
Axes of the slice: x: 4 (x_hi: 2, x_lo: 2; x = x_hi * 2 + x_lo), y: 8, z: 8, core: 2. Of those that a mesh axis runs over, the one named last changes fastest.
Arguments:
- query_latent_rows: bfloat16 [2, 4096, 1536], P('dp', 'ctx'), may hold values from -6 to 6
- latent: bfloat16 [2, 4096, 576], P('dp', 'ctx'), may hold values from -6 to 6
- wq_b: bfloat16 [48, 1536, 192], P('head', 'ctx'), may hold values from -5 to 5
- key_up_weight: bfloat16 [48, 512, 128], P('head', 'ctx'), may hold values from -0.5 to 0.5
- value_up_weight: bfloat16 [48, 512, 128], P('head', 'ctx'), may hold values from -0.25 to 0.25
- tau: int32 [48], P('head'), may hold values from 1 to 2
Outputs:
- attention: bfloat16 [2, 4096, 6144], P('dp', 'ctx', 'head')
- new_wq: bfloat16 [48, 1536, 192], P('head', 'ctx')
- new_uk: bfloat16 [48, 512, 128], P('head', 'ctx')
The draws below stay inside these ranges and needn't reach their ends.
All inputs are finite; a program needn't handle non-finite values.
Results may differ from the reference program's by a relative error of at most 0.017.
The reference program's roundings to bfloat16 on the way count: a program that leaves them out, or rounds other values in their place, can miss the bound.
Values may be sent and summed in bfloat16 or wider, within the bound.
A program may use at most 64 MiB of HBM per device.

```python
import math
import jax
import jax.numpy as jnp
from jax import lax

QUERY_LATENT = 1536
KEY_VALUE_LATENT = 512
PLAIN_HEAD_WIDTH = 128
ROTARY_WIDTH = 64
VALUE_HEAD_WIDTH = 128
HEAD_COUNT = 48
SEQUENCE_COUNT = 2
SEQUENCE_LENGTH = 4096
LAT = 576


def draw_wq_b(key, part):
    key = jax.random.fold_in(key, 7)
    scale_key, key_value_pair = jax.random.split(key)
    spread_rows = jnp.exp(jax.random.uniform(scale_key, (HEAD_COUNT, 1, 1), jnp.float32, jnp.log(1.0), jnp.log(3.0)))
    value_rows = jnp.clip(jax.random.normal(key_value_pair, (HEAD_COUNT, QUERY_LATENT, PLAIN_HEAD_WIDTH + ROTARY_WIDTH), jnp.float32), -3.0, 3.0)
    attention_weights = value_rows * spread_rows / jnp.sqrt(jnp.float32(QUERY_LATENT))
    return jnp.clip(attention_weights, -5.0, 5.0).astype(jnp.bfloat16)


def touch_ends(array, key, low, top_value):
    place = [jax.random.randint(jax.random.fold_in(key, axis), (), 0, length) for axis, length in enumerate(array.shape)]
    main_axis = array.shape.index(max(array.shape))
    beside = place[:main_axis] + [(place[main_axis] + 1) % array.shape[main_axis]] + place[main_axis + 1:]
    return array.at[tuple(place)].set(low).at[tuple(beside)].set(top_value)


def block_scale(key, dims, cuts, least, largest):
    def one(axis_at, blocks):
        heights = jax.random.uniform(jax.random.fold_in(jax.random.fold_in(key, 6), axis_at), (blocks,), jnp.float32, least / len(cuts), largest / len(cuts))
        return jnp.repeat(jnp.exp(heights), dims[axis_at] // blocks).reshape((-1,) + (1,) * (len(dims) - axis_at - 1))

    level = one(*cuts[0])
    for cut in cuts[1:]:
        level = level * one(*cut)
    return level


def normal_values(stream_key, extent, width, most, pieces=(), kind=jnp.bfloat16):
    array = width * jax.random.normal(stream_key, extent, jnp.float32)
    if pieces:
        array = array * block_scale(stream_key, extent, pieces, -0.22, 0.18)
    return jnp.clip(array, -most, most).astype(kind)


def setup_inputs(seed: int = 0) -> dict:
    splits = jax.random.split(jax.random.key(seed), 7)
    query_latent_rows = normal_values(splits[0], (SEQUENCE_COUNT, SEQUENCE_LENGTH, QUERY_LATENT), 1.0, 6.0, ((0, 2), (1, 32)))
    latent = normal_values(splits[1], (SEQUENCE_COUNT, SEQUENCE_LENGTH, LAT), 1.0, 6.0, ((0, 2), (1, 32)))
    wq_b = draw_wq_b(jax.random.fold_in(splits[6], 71), 0)
    key_up_weight = normal_values(splits[3], (HEAD_COUNT, KEY_VALUE_LATENT, PLAIN_HEAD_WIDTH), PLAIN_HEAD_WIDTH ** -0.5, 0.5, ((0, 8), (1, 32)))
    value_up_weight = normal_values(splits[4], (HEAD_COUNT, KEY_VALUE_LATENT, VALUE_HEAD_WIDTH), KEY_VALUE_LATENT ** -0.5, 0.25, ((0, 8), (1, 32)))
    tau = touch_ends(jax.random.randint(splits[5], (HEAD_COUNT,), 1, 3), jax.random.fold_in(splits[5], 1), 1, 2).astype(jnp.int32)
    return dict(query_latent_rows=query_latent_rows, latent=latent, wq_b=wq_b, key_up_weight=key_up_weight, value_up_weight=value_up_weight, tau=tau)


def rotate(value_rows, positions):
    half = value_rows.shape[-1] // 2
    freq = 50000.0 ** (-2.0 * jnp.arange(half, dtype=jnp.float32) / value_rows.shape[-1])
    angle = positions.astype(jnp.float32)[:, None] * freq[None, :]
    cosine = jnp.cos(angle)[:, None, :]
    sine = jnp.sin(angle)[:, None, :]
    first = value_rows[..., :half]
    second = value_rows[..., half:]
    return jnp.concatenate([first * cosine - second * sine, second * cosine + first * sine], -1)

def reference(query_latent_rows, latent, wq_b, key_up_weight, value_up_weight, tau):
    seqs = query_latent_rows.shape[0]
    length = query_latent_rows.shape[1]
    heads = wq_b.shape[0]
    nope = key_up_weight.shape[2]
    key_value_latent = key_up_weight.shape[1]
    vd = value_up_weight.shape[2]
    qk = wq_b.shape[2]
    block = math.gcd(length, 512)
    positions = jnp.arange(length, dtype=jnp.int32)
    outputs = []
    peaks = []
    for seq in range(seqs):
        query = jnp.einsum('tr,hrc->thc', query_latent_rows[seq].astype(jnp.float32), wq_b.astype(jnp.float32))
        q_nope = query[..., :nope].astype(jnp.bfloat16)
        q_lat = jnp.einsum('thn,hkn->thk', q_nope.astype(jnp.float32), key_up_weight.astype(jnp.float32))
        q_rot = rotate(query[..., nope:], positions)
        q_full = (jnp.concatenate([q_lat, q_rot], -1) * qk ** (-0.5)).astype(jnp.bfloat16)
        q_heads = jnp.transpose(q_full, (1, 0, 2))
        key_rows = latent[seq]

        def one_head(operands):
            q_head, value_map = operands
            q_blocks = q_head.reshape(length // block, block, q_head.shape[-1])
            starts = jnp.arange(length // block, dtype=jnp.int32) * block

            def one_block(pair):
                q_block, start = pair
                score = jnp.dot(q_block, key_rows.T, preferred_element_type=jnp.float32)
                rows = start + jnp.arange(block, dtype=jnp.int32)
                mask = positions[None, :] <= rows[:, None]
                score = jnp.where(mask, score, jnp.float32(-1e+30))
                row_max = lax.optimization_barrier(jnp.max(score, -1))
                exponent_terms = jnp.where(mask, jnp.exp(score - row_max[:, None]), jnp.float32(0.0))
                total = lax.optimization_barrier(jnp.sum(exponent_terms, -1))
                mixed_output = jnp.dot(exponent_terms.astype(jnp.bfloat16), key_rows[:, :key_value_latent], preferred_element_type=jnp.float32)
                mixed_output = (mixed_output / total[:, None]).astype(jnp.bfloat16)
                out = jnp.dot(mixed_output, value_map, preferred_element_type=jnp.float32).astype(jnp.bfloat16)
                return (out, jnp.max(row_max))
            outs, maxima = lax.map(one_block, (q_blocks, starts))
            return (outs.reshape(length, vd), jnp.max(maxima))
        head_out, head_peak = lax.map(one_head, (q_heads, value_up_weight))
        outputs.append(jnp.transpose(head_out, (1, 0, 2)).reshape(length, heads * vd))
        peaks.append(head_peak)
    attention = jnp.stack(outputs, 0)
    peak = lax.optimization_barrier(jnp.max(jnp.stack(peaks, 0), 0))
    limit = tau.astype(jnp.float32)
    gamma = limit / jnp.maximum(peak, limit)
    root = jnp.sqrt(gamma)
    wq32 = wq_b.astype(jnp.float32)
    new_wq = jnp.concatenate([wq32[..., :nope] * root[:, None, None], wq32[..., nope:] * gamma[:, None, None]], -1).astype(jnp.bfloat16)
    new_uk = (key_up_weight.astype(jnp.float32) * root[:, None, None]).astype(jnp.bfloat16)
    return (attention, new_wq, new_uk)
```

```python
import functools

import jax
import jax.numpy as jnp
from jax import lax
from jax.experimental import pallas as pl
from jax.experimental.pallas import tpu as pltpu
from jax.sharding import PartitionSpec as P

MESH = pl.DeviceIdType.MESH
F32 = jnp.float32
BF16 = jnp.bfloat16
LOW = -1e30

HEADS = 6
ROWS = 128
NOPE = 128
ROT = 64
LAT = 512
KEYW = 640
RING = 8
CHIPS = 16
GROUP = 4
GROUPS = CHIPS // GROUP
SLICE = ROWS // RING
WQW = HEADS * (NOPE + ROT)
UPW = HEADS * NOPE
QROWS = HEADS * ROWS
CHUNK = 2


def kernel(
    x_ref, lat_ref, wq_ref, uk_ref, uv_ref, tau_ref,
    att_ref, nwq_ref, nuk_ref,
    wq, uk, uv, keys, qf, mx, tot, acc, pk,
    l1_s, l1_r, wy_s, wy_r, wx_s, wx_r, ws_s, ws_r, z_s, z_r, ks_s, ks_r, pk_s, pk_r,
):
    dp = lax.axis_index("dp")
    ctx = lax.axis_index("ctx")
    z = lax.axis_index("head")
    core = lax.rem(ctx, 2)
    chip = ctx // 2
    xlo = chip // RING
    y = lax.rem(chip, RING)

    def wrap(v):
        return lax.rem(v + 2 * RING, RING)

    def dev(d, xl, yy, c, zz):
        return (d, (xl * RING + yy) * 2 + c, zz)

    sibling = dev(dp, xlo, y, 1 - core, z)
    y_next = (dev(dp, xlo, wrap(y + 1), core, z), dev(dp, xlo, wrap(y - 1), core, z))
    z_next = (dev(dp, xlo, y, core, wrap(z + 1)), dev(dp, xlo, y, core, wrap(z - 1)))
    x_up = dev(lax.rem(dp + xlo, 2), 1 - xlo, y, core, z)
    x_down = dev(lax.rem(dp + 1 + xlo, 2), 1 - xlo, y, core, z)

    def l1_dev(dx, dy):
        return dev(dp, lax.rem(xlo + dx, 2), wrap(y + dy), core, z)

    def plane_dev(k):
        return dev(
            lax.rem(dp + k // 4, 2), lax.rem(xlo + (k // 2) % 2, 2), y, lax.rem(core + k % 2, 2), z
        )

    barrier = pltpu.get_barrier_semaphore()
    partners = [l1_dev(dx, dy) for dx in range(2) for dy in range(RING) if dx or dy]
    partners += [plane_dev(k) for k in range(1, 8) if k != 2]
    partners += list(z_next)
    for partner in partners:
        pl.semaphore_signal(barrier, inc=1, device_id=partner, device_id_type=MESH)

    for h in range(HEADS):
        wq[chip, core, :, h * NOPE : (h + 1) * NOPE] = wq_ref[h, :, :NOPE]
        uk[chip, core, :, h * NOPE : (h + 1) * NOPE] = uk_ref[h]
        uv[chip, core, :, h * NOPE : (h + 1) * NOPE] = uv_ref[h]
    for j in range(HEADS // 2):
        pair = jnp.concatenate([wq_ref[2 * j, :, NOPE:], wq_ref[2 * j + 1, :, NOPE:]], -1)
        wq[chip, core, :, UPW + j * 128 : UPW + (j + 1) * 128] = pair
    own_rows = pl.ds(pl.multiple_of(z * SLICE, SLICE), SLICE)
    own_slice = lat_ref[0, own_rows, :]
    keys[chip, core, own_rows, :] = jnp.concatenate(
        [own_slice, jnp.zeros((SLICE, KEYW - LAT - ROT), BF16)], -1
    )

    pl.semaphore_wait(barrier, len(partners))

    sent = []

    def guarded(cond, f):
        if cond is None:
            f()
        else:
            pl.when(cond)(f)

    def send(make, cond=None):
        sent.append((cond, make))
        guarded(cond, lambda: make().start())

    def arrive(make, cond=None):
        guarded(cond, lambda: make().wait_recv())

    def copy(ref, ssem, rsem, to):
        return lambda: pltpu.make_async_remote_copy(
            src_ref=ref(), dst_ref=ref(), send_sem=ssem, recv_sem=rsem, device_id=to, device_id_type=MESH
        )

    def slice_of(p0, n, zz):
        rows = pl.ds(pl.multiple_of(zz * SLICE, SLICE), SLICE)
        return keys.at[pl.ds(p0, n), core, rows, :]

    my_group = chip // GROUP
    for dx in (0, 1):
        for dy in (1, 7, 2, 6, 3, 5, 4, 0):
            if dx == 0 and dy == 0:
                continue
            there = lax.rem(xlo + dx, 2) * RING + wrap(y + dy)
            i = dx * RING + dy
            send(
                copy(lambda: slice_of(chip, 1, z), l1_s.at[i], l1_r.at[i], l1_dev(dx, dy)),
                my_group <= there // GROUP,
            )

    def need(g):
        return g * GROUP <= chip

    def l1_wait(g):
        for p in range(g * GROUP, (g + 1) * GROUP):
            i = lax.rem(xlo + p // RING, 2) * RING + wrap(y - p % RING)
            arrive(
                copy(lambda: slice_of(p, 1, z), l1_s.at[i], l1_r.at[i], sibling),
                jnp.logical_and(need(g), chip != p),
            )

    def z_copy(g, way, s):
        sign = 1 if way == 0 else -1
        half = GROUP // 2
        p0, n = (g * GROUP, GROUP) if s < 4 else (g * GROUP + way * half, half)
        return lambda src: copy(
            lambda: slice_of(p0, n, wrap(z - sign * src)), z_s.at[way, g, s - 1], z_r.at[way, g, s - 1], z_next[way]
        )

    def z_send(g, s):
        for way in (0, 1):
            send(z_copy(g, way, s)(s - 1), need(g))

    def z_wait(g, s):
        for way in (0, 1):
            arrive(z_copy(g, way, s)(s), need(g))

    def z_step(g, s):
        z_wait(g, s)
        if s < 4:
            z_send(g, s + 1)
        else:
            send(
                copy(lambda: keys.at[pl.ds(g * GROUP, GROUP), core], ks_s.at[g], ks_r.at[g], sibling),
                need(g),
            )

    def group_wait(g):
        arrive(
            copy(lambda: keys.at[pl.ds(g * GROUP, GROUP), 1 - core], ks_s.at[g], ks_r.at[g], sibling),
            need(g),
        )

    arrays = (wq, uk, uv)
    ORDER = (0, -1, -2, -3, -4, 3, 2, 1)

    def piece(a, xl, slot, c):
        p = xl * RING + wrap(y + ORDER[slot])
        return lambda: arrays[a].at[p, c]

    def wy_copy(a, way, s, src_slot):
        return copy(piece(a, xlo, src_slot, core), wy_s.at[way, s - 1, a], wy_r.at[way, s - 1, a], y_next[way])

    def wx_copy(part, slot, xl):
        p = xl * RING + wrap(y + ORDER[slot])
        ref = (
            lambda: wq.at[p, core, pl.ds(0, 32), :],
            lambda: wq.at[p, core, pl.ds(32, 16), :],
            lambda: uk.at[p, core],
            lambda: uv.at[p, core],
        )[part]
        return copy(ref, wx_s.at[slot, part], wx_r.at[slot, part], x_up if part == 0 else x_down)

    def ws_copy(a, column, slot, c):
        xl = xlo if column == 0 else 1 - xlo
        i = column * 8 + slot
        return copy(piece(a, xl, slot, c), ws_s.at[i, a], ws_r.at[i, a], sibling)

    def spread(a, slot):
        for part in (0, 1) if a == 0 else (a + 1,):
            send(wx_copy(part, slot, xlo))
        send(ws_copy(a, 0, slot, core))

    def w_begin():
        for a in range(3):
            for way in (0, 1):
                send(wy_copy(a, way, 1, 0))
            spread(a, 0)

    def w_step(s):
        for way in (0, 1):
            slot = s if way == 0 else 8 - s
            for a in range(3):
                if s == 4 and (a == 0) != (way == 0):
                    continue
                arrive(wy_copy(a, way, s, slot))
                if s < 3 or (s == 3 and (a == 0) == (way == 0)):
                    send(wy_copy(a, way, s + 1, slot))
                spread(a, slot)

    def w_across(slot):
        for a in range(3):
            for part in (0, 1) if a == 0 else (a + 1,):
                arrive(wx_copy(part, slot, 1 - xlo))
            send(ws_copy(a, 1, slot, core))

    def w_have(a):
        for column in (0, 1):
            for slot in range(8):
                arrive(ws_copy(a, column, slot, 1 - core))

    def project():
        xx = x_ref[0]
        w = wq[...].reshape(CHIPS * 2 * 48, WQW)
        query = jnp.dot(xx, w, preferred_element_type=F32)
        lane = lax.broadcasted_iota(jnp.int32, (ROWS, 128), 1)
        row = lax.broadcasted_iota(jnp.int32, (ROWS, 128), 0)
        half = ROT // 2
        expo = (-2.0 / ROT) * lax.rem(lane, half).astype(F32)
        freq = jnp.exp(expo * jnp.log(F32(50000.0)))
        angle = (ctx * ROWS + row).astype(F32) * freq
        first = lax.rem(lane, ROT) < half
        cosine = jnp.cos(angle)
        sine = jnp.sin(angle)
        sine = jnp.where(first, -sine, sine)
        scale = F32((NOPE + ROT) ** -0.5)
        ukw = uk[...].reshape(LAT, UPW)
        for j in range(HEADS // 2):
            q = query[:, UPW + j * 128 : UPW + (j + 1) * 128]
            other = jnp.where(first, pltpu.roll(q, 128 - half, 1), pltpu.roll(q, half, 1))
            rot = ((q * cosine + other * sine) * scale).astype(F32)
            left = jnp.where(lane < ROT, rot, 0.0)
            right = jnp.where(lane < ROT, pltpu.roll(rot, ROT, 1), 0.0)
            for h, part in ((2 * j, left), (2 * j + 1, right)):
                nope = query[:, h * NOPE : (h + 1) * NOPE].astype(BF16)
                q_lat = lax.dot_general(
                    nope, ukw[:, h * NOPE : (h + 1) * NOPE], (((1,), (1,)), ((), ())), preferred_element_type=F32
                )
                qf[pl.ds(h * ROWS, ROWS), :LAT] = (q_lat * scale).astype(BF16)
                qf[pl.ds(h * ROWS, ROWS), LAT:] = part.astype(BF16)
        mx[...] = jnp.full_like(mx, LOW)
        tot[...] = jnp.zeros_like(tot)
        acc[...] = jnp.zeros_like(acc)

    BLK = 384

    def attend(j):
        kc = keys[pl.ds(CHUNK * j, CHUNK)].reshape(CHUNK * 2 * ROWS, KEYW)
        width = CHUNK * 2 * ROWS
        for r in range(QROWS // BLK):
            rows = pl.ds(r * BLK, BLK)
            s = lax.dot_general(qf[rows, :], kc, (((1,), (1,)), ((), ())), preferred_element_type=F32)
            t = ctx * ROWS + lax.rem(lax.broadcasted_iota(jnp.int32, (BLK, width), 0), ROWS)
            u = j * width + lax.broadcasted_iota(jnp.int32, (BLK, width), 1)
            s = jnp.where(u <= t, s, LOW)
            old = mx[rows, :]
            new = jnp.maximum(old, jnp.max(s, -1, keepdims=True))
            mx[rows, :] = new
            alpha = jnp.exp(old - new)
            parts = [jnp.exp(s[:, i * 128 : (i + 1) * 128] - new) for i in range(width // 128)]
            tot[rows, :] = tot[rows, :] * alpha + functools.reduce(jnp.add, parts)
            prob = jnp.concatenate([p.astype(BF16) for p in parts], -1)
            add = jnp.dot(prob, kc[:, :LAT], preferred_element_type=F32)
            acc[rows, :] = acc[rows, :] * jnp.concatenate([alpha] * (LAT // 128), -1) + add

    def attend_group(g):
        per = GROUP // CHUNK

        def body(j, _):
            @pl.when(CHUNK * j <= chip)
            def _():
                attend(j)

            return 0

        lax.fori_loop(g * per, (g + 1) * per, body, 0)

    def peak_copy(stage, k):
        if stage == 0:
            to = plane_dev(k)
        else:
            to = dev(dp, xlo, wrap(y + k), core, z)
        return lambda: pltpu.make_async_remote_copy(
            src_ref=pk.at[stage, 0], dst_ref=pk.at[stage, k], send_sem=pk_s.at[stage, k],
            recv_sem=pk_r.at[stage, k], device_id=to, device_id_type=MESH,
        )

    def peak_begin():
        for h in range(HEADS):
            pk[0, 0, h : h + 1, :] = jnp.max(mx[pl.ds(h * ROWS, ROWS), :], 0, keepdims=True)
        pk[0, 0, HEADS:, :] = jnp.full((8 - HEADS, 128), LOW, F32)
        for k in range(1, 8):
            send(peak_copy(0, k))

    def peak_next():
        for k in range(1, 8):
            arrive(peak_copy(0, k))
        pk[1, 0] = jnp.max(pk[0], 0)
        for k in range(1, 8):
            send(peak_copy(1, k))

    def finish():
        for k in range(1, 8):
            arrive(peak_copy(1, k))
        peak = jnp.max(pk[1], 0)
        for h in range(HEADS):
            limit = jnp.full((1, 128), tau_ref[h].astype(F32), F32)
            gamma = limit / jnp.maximum(peak[h : h + 1, :], limit)
            root = jnp.sqrt(gamma)
            nwq_ref[h, :, :NOPE] = (wq_ref[h, :, :NOPE].astype(F32) * root).astype(BF16)
            nwq_ref[h, :, NOPE:] = (wq_ref[h, :, NOPE:].astype(F32) * gamma[:, :ROT]).astype(BF16)
            nuk_ref[h] = (uk_ref[h].astype(F32) * root).astype(BF16)

    def output():
        uvw = uv[...].reshape(LAT, UPW)
        for h in range(HEADS):
            rows = pl.ds(h * ROWS, ROWS)
            total = jnp.sum(tot[rows, :], -1, keepdims=True)
            mixed = (acc[rows, :] / total).astype(BF16)
            att_ref[0, :, h * NOPE : (h + 1) * NOPE] = jnp.dot(
                mixed, uvw[:, h * NOPE : (h + 1) * NOPE], preferred_element_type=F32
            ).astype(BF16)

    w_begin()
    for g in (0, 1):
        l1_wait(g)
        z_send(g, 1)
    w_step(1)
    w_across(0)
    z_step(0, 1)
    z_step(1, 1)
    w_step(2)
    for slot in (1, 7):
        w_across(slot)
    z_step(0, 2)
    z_step(1, 2)
    w_step(3)
    for slot in (2, 6):
        w_across(slot)
    z_step(0, 3)
    for g in (2, 3):
        l1_wait(g)
    z_send(2, 1)
    z_step(1, 3)
    z_send(3, 1)
    w_step(4)
    for slot in (3, 5, 4):
        w_across(slot)
    z_step(0, 4)
    z_step(1, 4)
    z_step(2, 1)
    w_have(0)
    w_have(1)
    z_step(3, 1)
    project()
    z_step(2, 2)
    z_step(3, 2)
    group_wait(0)
    attend_group(0)
    z_step(2, 3)
    z_step(3, 3)
    group_wait(1)
    attend_group(1)
    z_step(2, 4)
    z_step(3, 4)
    group_wait(2)
    attend_group(2)
    group_wait(3)
    attend_group(3)
    peak_begin()
    w_have(2)
    output()
    peak_next()
    finish()
    for cond, make in sent:
        guarded(cond, lambda: make().wait_send())


def shards(query_latent_rows, latent, wq_b, key_up_weight, value_up_weight, tau):
    dma = pltpu.SemaphoreType.DMA
    vmem = pl.BlockSpec(memory_space=pltpu.VMEM)
    return pl.pallas_call(
        kernel,
        out_shape=(
            jax.ShapeDtypeStruct((1, ROWS, UPW), BF16),
            jax.ShapeDtypeStruct(wq_b.shape, BF16),
            jax.ShapeDtypeStruct(key_up_weight.shape, BF16),
        ),
        in_specs=[vmem] * 5 + [pl.BlockSpec(memory_space=pltpu.SMEM)],
        out_specs=(vmem,) * 3,
        scratch_shapes=[
            pltpu.VMEM((CHIPS, 2, 48, WQW), BF16),
            pltpu.VMEM((CHIPS, 2, 16, UPW), BF16),
            pltpu.VMEM((CHIPS, 2, 16, UPW), BF16),
            pltpu.VMEM((CHIPS, 2, ROWS, KEYW), BF16),
            pltpu.VMEM((QROWS, KEYW), BF16),
            pltpu.VMEM((QROWS, 128), F32),
            pltpu.VMEM((QROWS, 128), F32),
            pltpu.VMEM((QROWS, LAT), F32),
            pltpu.VMEM((2, 8, 8, 128), F32),
            dma((16,)), dma((16,)),
            dma((2, 4, 3)), dma((2, 4, 3)),
            dma((8, 4)), dma((8, 4)),
            dma((16, 3)), dma((16, 3)),
            dma((2, GROUPS, 4)), dma((2, GROUPS, 4)),
            dma((GROUPS,)), dma((GROUPS,)),
            dma((2, 8)), dma((2, 8)),
        ],
        compiler_params=pltpu.CompilerParams(
            collective_id=0, has_side_effects=True, vmem_limit_bytes=48 * 1024 * 1024
        ),
        name="latent_attention",
    )(query_latent_rows, latent, wq_b, key_up_weight, value_up_weight, tau)


def solution(mesh):
    in_specs = (
        P("dp", "ctx", None),
        P("dp", "ctx", None),
        P("head", "ctx", None),
        P("head", "ctx", None),
        P("head", "ctx", None),
        P("head"),
    )
    out_specs = (P("dp", "ctx", "head"), P("head", "ctx", None), P("head", "ctx", None))
    return jax.shard_map(shards, mesh=mesh, in_specs=in_specs, out_specs=out_specs, check_vma=False)
```

```python
import functools

import jax
import jax.numpy as jnp
from jax import lax
from jax.experimental import pallas as pl
from jax.experimental.pallas import tpu as pltpu
from jax.sharding import PartitionSpec as P

MESH = pl.DeviceIdType.MESH
F32 = jnp.float32
BF16 = jnp.bfloat16
LOW = -1e30

HEADS = 6
HALF = 3
ROWS = 128
TOKS = 2 * ROWS
NOPE = 128
ROT = 64
LAT = 512
KEYW = LAT + ROT
RING = 8
CHIPS = 16
QUARTER = KEYW // 4
WROW = 48
UROW = 16
UPW = HALF * NOPE
WQW = UPW + 2 * 128
QROWS = HALF * TOKS
CHUNK = 2
WIDTH = CHUNK * TOKS
PLANE = 32


def kernel(
    x_ref, lat_ref, wq_ref, uk_ref, uv_ref, tau_ref,
    att_ref, nwq_ref, nuk_ref,
    wq, uk, uv, keys, xs, wq_in, uk_in, uv_in, wq_st, uk_st, uv_st, qf, score, mx, tot, acc, pk, pk2, att_out, att_in,
    ld_s, in_s, in_r, l1_s, l1_r, lx_s, wy_s, wy_r, wx_s, wx_r, z_s, z_r, ks_s, ks_r, pk_s, pk_r, fin_s, fin_r,
):
    dp = lax.axis_index("dp")
    ctx = lax.axis_index("ctx")
    z = lax.axis_index("head")
    core = lax.rem(ctx, 2)
    chip = ctx // 2
    xlo = chip // RING
    y = lax.rem(chip, RING)

    def wrap(v):
        return lax.rem(v + 2 * RING, RING)

    def dev(d, xl, yy, c, zz):
        return (d, (xl * RING + yy) * 2 + c, zz)

    sibling = dev(dp, xlo, y, 1 - core, z)
    y_next = (dev(dp, xlo, wrap(y + 1), core, z), dev(dp, xlo, wrap(y - 1), core, z))
    z_next = (dev(dp, xlo, y, core, wrap(z + 1)), dev(dp, xlo, y, core, wrap(z - 1)))
    def plane_dev(k):
        return dev(lax.rem(dp + k // 16, 2), lax.rem(xlo + (k // 8) % 2, 2), wrap(y + k % 8), core, z)

    def lay_out(c, wq_to, uk_to, uv_to):
        for i in range(HALF):
            h = HALF * c + i
            cols = slice(i * NOPE, (i + 1) * NOPE)
            wq_to[:, cols] = wq_in[h, :, :NOPE]
            uk_to[:, cols] = uk_in[h]
            uv_to[:, cols] = uv_in[h]
        rope = [wq_in[HALF * c + i, :, NOPE:] for i in range(HALF)]
        wq_to[:, UPW : UPW + 128] = jnp.concatenate(rope[:2], -1)
        wq_to[:, UPW + 128 :] = jnp.concatenate([rope[2], jnp.zeros((WROW, ROT), BF16)], -1)

    def wrows(c):
        return pl.ds(pl.multiple_of(c * WROW, WROW), WROW)

    def urows(c):
        return pl.ds(pl.multiple_of(c * UROW, UROW), UROW)


    def quarter(zz):
        return pl.ds(pl.multiple_of(lax.rem(zz + 8, 4) * QUARTER, QUARTER), QUARTER)

    loads = [
        pltpu.make_async_copy(wq_ref, wq_in, ld_s.at[0]),
        pltpu.make_async_copy(uk_ref, uk_in, ld_s.at[1]),
        pltpu.make_async_copy(uv_ref, uv_in, ld_s.at[2]),
        pltpu.make_async_copy(x_ref.at[0], xs.at[core], ld_s.at[3]),
        pltpu.make_async_copy(lat_ref.at[0], keys.at[chip, core], ld_s.at[4]),
    ]
    for load in loads:
        load.start()
    barrier = pltpu.get_barrier_semaphore()
    partners = [plane_dev(k) for d in (4, 3, 5, 2, 6, 1, 7, 0) for k in range(1, PLANE) if k % 8 == d]
    partners += [*z_next, sibling]
    for partner in partners:
        pl.semaphore_signal(barrier, inc=1, device_id=partner, device_id_type=MESH)
    for load in loads:
        load.wait()
    lay_out(1 - core, wq_st, uk_st, uv_st)
    lay_out(core, wq.at[chip, wrows(core)], uk.at[chip, urows(core)], uv.at[chip, urows(core)])
    pl.semaphore_wait(barrier, len(partners))

    sent = []

    def guarded(cond, f):
        if cond is None:
            f()
        else:
            pl.when(cond)(f)

    def send(make, cond=None):
        sent.append((cond, make))
        guarded(cond, lambda: make().start())

    def arrive(make, cond=None):
        guarded(cond, lambda: make().wait_recv())

    def copy(src, dst, ssem, rsem, to):
        return lambda: pltpu.make_async_remote_copy(
            src_ref=src(), dst_ref=dst(), send_sem=ssem, recv_sem=rsem, device_id=to, device_id_type=MESH
        )

    def in_copy(i, c):
        src, dst = (
            (lambda: wq_st, lambda: wq.at[chip, wrows(c)]),
            (lambda: uk_st, lambda: uk.at[chip, urows(c)]),
            (lambda: uv_st, lambda: uv.at[chip, urows(c)]),
            (lambda: xs.at[c], lambda: xs.at[c]),
        )[i]
        return copy(src, dst, in_s.at[i], in_r.at[i], sibling)

    ORDER = (0, -1, -2, -3, -4, 3, 2, 1)
    ACROSS = ((0, 0, 1, 1, 1, 1, 0, 1), (0, 1, 0, 1, 0, 1, 0, 1))

    def piece(a, xl, slot):
        p = xl * RING + wrap(y + ORDER[slot])
        if a < 6:
            src = core if a < 3 else 1 - core
            rows = pl.ds(pl.multiple_of(src * WROW + (a % 3) * 16, 16), 16)
            return lambda: wq.at[p, rows]
        return (lambda: uk.at[p]) if a == 6 else (lambda: uv.at[p])

    def wy_copy(a, way, s, slot):
        ref = piece(a, xlo, slot)
        return copy(ref, ref, wy_s.at[way, s - 1, a], wy_r.at[way, s - 1, a], y_next[way])

    def wx_copy(a, slot, xl, turn=0):
        ref = piece(a, xl, slot)
        down = jnp.where(xlo == 0, ACROSS[0][a], ACROSS[1][a])
        to = dev(lax.rem(dp + xlo + down, 2), 1 - xlo, wrap(y + turn), core, z)
        index = slot if turn == 0 else 4
        return copy(ref, ref, wx_s.at[index, a], wx_r.at[index, a], to)

    def w_begin(a):
        for way in (0, 1):
            send(wy_copy(a, way, 1, 0))
        send(wx_copy(a, 0, xlo))

    def w_step(s, parts=range(8)):
        for a in parts:
            for way in (0, 1):
                slot = s if way == 0 else 8 - s
                if s == 4 and a % 2 != way:
                    continue
                arrive(wy_copy(a, way, s, slot))
                if s < 3:
                    send(wy_copy(a, way, s + 1, slot))
                if s == 3 and a % 2 == way:
                    send(wx_copy(a, slot, xlo, 1 if way == 0 else -1))
                    send(wy_copy(a, way, s + 1, slot))
                if s < 4:
                    send(wx_copy(a, slot, xlo))

    def w_have(parts):
        for slot in range(8):
            for a in parts:
                arrive(wx_copy(a, slot, 1 - xlo))

    def keys_of(p, zz):
        return lambda: keys.at[p, core, quarter(zz), :]

    left = xlo == 0
    right = xlo == 1
    source = [chip] + [xlo * RING + wrap(y - k) for k in range(1, RING)] + list(range(RING))
    wanted = [None] + [y >= k for k in range(1, RING)] + [right] * RING

    def l1_copy(k):
        p = chip if k == 0 else source[k]
        return copy(keys_of(p, z), keys_of(p, z), l1_s.at[0], l1_r.at[k], plane_dev(8))

    def l1_begin():
        for k in (1, 7, 2, 6, 3, 5, 4):
            ref = keys_of(chip, z)
            send(
                copy(ref, ref, l1_s.at[k], l1_r.at[k], plane_dev(k)),
                jnp.logical_or(left, y + k < RING),
            )
        across(chip, left)

    def across(p, cond):
        ref = keys_of(p, z)
        i = 8 + lax.rem(p, RING)
        send(copy(ref, ref, lx_s.at[i - 8], l1_r.at[i], plane_dev(8)), cond)

    def l1_wait(k):
        arrive(l1_copy(k), jnp.logical_or(left, wanted[k]) if k < 8 else wanted[k])
        if k < 8:
            across(source[k], left)
        for way in (0, 1):
            send(z_copy(k, way, 1), wanted[k])

    def z_copy(k, way, s, src=None):
        sign = 1 if way == 0 else -1
        ref = keys_of(source[k], z - sign * (s - 1 if src is None else src))
        return copy(ref, ref, z_s.at[way, s - 1, k], z_r.at[way, s - 1, k], z_next[way])

    def z_turn(k):
        for way in (0, 1):
            arrive(z_copy(k, way, 1, 1), wanted[k])
        send(z_copy(k, k % 2, 2), wanted[k])

    def ks_copy(p, c):
        ref = lambda: keys.at[p, c]
        return copy(ref, ref, ks_s.at[p], ks_r.at[p], sibling)

    def z_end(k):
        if k:
            arrive(z_copy(k, k % 2, 2, 2), wanted[k])
        send(ks_copy(source[k], core), wanted[k])

    def chip_wait(p):
        arrive(ks_copy(p, 1 - core), p <= chip)

    def project():
        xx = xs[...].reshape(TOKS, 2 * CHIPS * WROW)
        w = wq[...].reshape(2 * CHIPS * WROW, WQW)
        query = jnp.dot(xx, w, preferred_element_type=F32)
        lane = lax.broadcasted_iota(jnp.int32, (TOKS, 128), 1)
        row = lax.broadcasted_iota(jnp.int32, (TOKS, 128), 0)
        half = ROT // 2
        expo = (-2.0 / ROT) * lax.rem(lane, half).astype(F32)
        freq = jnp.exp(expo * jnp.log(F32(50000.0)))
        angle = (chip * TOKS + row).astype(F32) * freq
        first = lax.rem(lane, ROT) < half
        cosine = jnp.cos(angle)
        sine = jnp.sin(angle)
        sine = jnp.where(first, -sine, sine)
        scale = F32((NOPE + ROT) ** -0.5)
        ukw = uk[...].reshape(LAT, UPW)
        rots = []
        for j in range(2):
            q = query[:, UPW + j * 128 : UPW + (j + 1) * 128]
            other = jnp.where(first, pltpu.roll(q, 128 - half, 1), pltpu.roll(q, half, 1))
            rots.append((q * cosine + other * sine) * scale)
        rots = [rots[0][:, :ROT], pltpu.roll(rots[0], ROT, 1)[:, :ROT], rots[1][:, :ROT]]
        for i in range(HALF):
            rows = pl.ds(i * TOKS, TOKS)
            nope = query[:, i * NOPE : (i + 1) * NOPE].astype(BF16)
            q_lat = lax.dot_general(
                nope, ukw[:, i * NOPE : (i + 1) * NOPE], (((1,), (1,)), ((), ())), preferred_element_type=F32
            )
            qf[rows, :LAT] = (q_lat * scale).astype(BF16)
            qf[rows, LAT:] = rots[i].astype(BF16)
        mx[...] = jnp.full_like(mx, LOW)

    def keys_at(j):
        at = [jnp.minimum(CHUNK * j + a, chip) for a in range(CHUNK)]
        return jnp.concatenate([keys[p, c] for p in at for c in range(2)], -1)

    def scores(j, masked):
        kt = keys_at(j)
        for i in range(HALF):
            rows = pl.ds(i * TOKS, TOKS)
            s = jnp.dot(qf[rows, :], kt, preferred_element_type=F32)
            if masked:
                t = (chip - CHUNK * j) * TOKS + lax.broadcasted_iota(jnp.int32, (TOKS, WIDTH), 0)
                s = jnp.where(lax.broadcasted_iota(jnp.int32, (TOKS, WIDTH), 1) <= t, s, LOW)
            score[j, rows, :] = s
            parts = [s[:, b * 128 : (b + 1) * 128] for b in range(WIDTH // 128)]
            mx[rows, :] = functools.reduce(jnp.maximum, parts, mx[rows, :])

    def scores_all():
        def body(j, _):
            for a in range(CHUNK):
                chip_wait(CHUNK * j + a)

            @pl.when(j < chip // CHUNK)
            def _():
                scores(j, False)

            @pl.when(j == chip // CHUNK)
            def _():
                scores(j, True)

            return 0

        lax.fori_loop(0, CHIPS // CHUNK, body, 0)

    def mix_all():
        mx[...] = jnp.broadcast_to(jnp.max(mx[...], -1, keepdims=True), mx.shape)
        tot[...] = jnp.zeros_like(tot)
        acc[...] = jnp.zeros_like(acc)

        def body(j, _):
            kt = keys_at(j)[:LAT]
            for i in range(HALF):
                rows = pl.ds(i * TOKS, TOKS)
                top = mx[rows, :]
                parts = [jnp.exp(score[j, rows, b * 128 : (b + 1) * 128] - top) for b in range(WIDTH // 128)]
                tot[rows, :] += functools.reduce(jnp.add, parts)
                prob = jnp.concatenate([p.astype(BF16) for p in parts], -1)
                acc[rows, :] += lax.dot_general(prob, kt, (((1,), (1,)), ((), ())), preferred_element_type=F32)
            return 0

        lax.fori_loop(0, chip // CHUNK + 1, body, 0)

    def peak_copy(k):
        return copy(lambda: pk.at[0], lambda: pk.at[k], pk_s.at[k], pk_r.at[k], plane_dev(k))

    def peak_begin():
        for i in range(HALF):
            pk[0, i : i + 1, :] = jnp.max(mx[pl.ds(i * TOKS, TOKS), :], 0, keepdims=True)
        pk[0, HALF:, :] = jnp.full((8 - HALF, 128), LOW, F32)
        for k in [k for d in (4, 3, 5, 2, 6, 1, 7, 0) for k in range(1, PLANE) if k % 8 == d]:
            send(peak_copy(k))

    def fin_copy(i, c):
        src, dst = (
            (lambda: pk2.at[c], lambda: pk2.at[c]),
            (lambda: att_out, lambda: att_in),
        )[i]
        return copy(src, dst, fin_s.at[i], fin_r.at[i], sibling)

    def peak_end():
        for k in range(1, PLANE):
            arrive(peak_copy(k))
        pk2[core] = jnp.max(pk[...], 0)
        send(fin_copy(0, core))

    def finish():
        arrive(fin_copy(0, 1 - core))
        for h in range(HEADS):
            peak = jnp.max(pk2[h // HALF, h % HALF : h % HALF + 1, :], -1, keepdims=True)
            limit = jnp.full((1, 128), tau_ref[h].astype(F32), F32)
            gamma = limit / jnp.maximum(peak, limit)
            root = jnp.sqrt(gamma)
            nwq_ref[h, :, :NOPE] = (wq_in[h, :, :NOPE].astype(F32) * root).astype(BF16)
            nwq_ref[h, :, NOPE:] = (wq_in[h, :, NOPE:].astype(F32) * gamma[:, :ROT]).astype(BF16)
            nuk_ref[h] = (uk_in[h].astype(F32) * root).astype(BF16)

    def output():
        uvw = uv[...].reshape(LAT, UPW)

        def of(c, i):
            rows = pl.ds(pl.multiple_of(i * TOKS + c * ROWS, ROWS), ROWS)
            total = jnp.sum(tot[rows, :], -1, keepdims=True)
            mixed = (acc[rows, :] / total).astype(BF16)
            w = uvw[:, i * NOPE : (i + 1) * NOPE]
            return jnp.dot(mixed, w, preferred_element_type=F32).astype(BF16)

        for i in range(HALF):
            att_out[:, i * NOPE : (i + 1) * NOPE] = of(1 - core, i)
        send(fin_copy(1, core))
        for i in range(HALF):
            att_ref[0, :, pl.ds(pl.multiple_of((core * HALF + i) * NOPE, NOPE), NOPE)] = of(core, i)

    def output_end():
        arrive(fin_copy(1, 1 - core))
        att_ref[0, :, pl.ds(pl.multiple_of((1 - core) * UPW, UPW), UPW)] = att_in[...]

    for i in range(4):
        send(in_copy(i, core))
    for a in range(3):
        w_begin(a)
    l1_begin()
    arrive(in_copy(0, 1 - core))
    for a in (3, 4, 5):
        w_begin(a)
    arrive(in_copy(1, 1 - core))
    w_begin(6)
    arrive(in_copy(2, 1 - core))
    w_begin(7)
    z_end(0)
    for k in (1, 7):
        l1_wait(k)
    w_step(1)
    for k in (2, 6, 3, 5, 4):
        l1_wait(k)
    w_step(2)
    for k in (1, 7, 2):
        z_turn(k)
    for k in range(8, 16):
        l1_wait(k)
    w_step(3)
    for k in (6, 3, 5, 4):
        z_turn(k)
    for k in (1, 7, 2, 6, 3):
        z_end(k)
    for k in (8, 9, 10, 11):
        z_turn(k)
    w_step(4)
    arrive(in_copy(3, 1 - core))
    for k in (12, 13, 14, 15):
        z_turn(k)
    for k in (5, 4, 8, 9, 10, 11):
        z_end(k)
    w_have(range(7))
    project()
    for k in (12, 13, 14, 15):
        z_end(k)
    scores_all()
    peak_begin()
    mix_all()
    w_have((7,))
    output()
    peak_end()
    output_end()
    finish()
    for cond, make in sent:
        guarded(cond, lambda: make().wait_send())


def shards(query_latent_rows, latent, wq_b, key_up_weight, value_up_weight, tau):
    dma = pltpu.SemaphoreType.DMA
    vmem = pl.BlockSpec(memory_space=pltpu.VMEM)
    hbm = pl.BlockSpec(memory_space=pltpu.HBM)
    return pl.pallas_call(
        kernel,
        out_shape=(
            jax.ShapeDtypeStruct((1, ROWS, HEADS * NOPE), BF16),
            jax.ShapeDtypeStruct(wq_b.shape, BF16),
            jax.ShapeDtypeStruct(key_up_weight.shape, BF16),
        ),
        in_specs=[hbm] * 5 + [pl.BlockSpec(memory_space=pltpu.SMEM)],
        out_specs=(vmem,) * 3,
        scratch_shapes=[
            pltpu.VMEM((CHIPS, 2 * WROW, WQW), BF16),
            pltpu.VMEM((CHIPS, 2 * UROW, UPW), BF16),
            pltpu.VMEM((CHIPS, 2 * UROW, UPW), BF16),
            pltpu.VMEM((CHIPS, 2, KEYW, ROWS), BF16),
            pltpu.VMEM((2, ROWS, 2 * CHIPS * WROW), BF16),
            pltpu.VMEM((HEADS, WROW, NOPE + ROT), BF16),
            pltpu.VMEM((HEADS, UROW, NOPE), BF16),
            pltpu.VMEM((HEADS, UROW, NOPE), BF16),
            pltpu.VMEM((WROW, WQW), BF16),
            pltpu.VMEM((UROW, UPW), BF16),
            pltpu.VMEM((UROW, UPW), BF16),
            pltpu.VMEM((QROWS, KEYW), BF16),
            pltpu.VMEM((CHIPS // CHUNK, QROWS, WIDTH), F32),
            pltpu.VMEM((QROWS, 128), F32),
            pltpu.VMEM((QROWS, 128), F32),
            pltpu.VMEM((QROWS, LAT), F32),
            pltpu.VMEM((PLANE, 8, 128), F32),
            pltpu.VMEM((2, 8, 128), F32),
            pltpu.VMEM((ROWS, UPW), BF16),
            pltpu.VMEM((ROWS, UPW), BF16),
            dma((5,)),
            dma((4,)), dma((4,)),
            dma((8,)), dma((16,)),
            dma((8,)),
            dma((2, 4, 8)), dma((2, 4, 8)),
            dma((8, 8)), dma((8, 8)),
            dma((2, 2, CHIPS)), dma((2, 2, CHIPS)),
            dma((CHIPS,)), dma((CHIPS,)),
            dma((PLANE,)), dma((PLANE,)),
            dma((2,)), dma((2,)),
        ],
        compiler_params=pltpu.CompilerParams(
            collective_id=0, has_side_effects=True, vmem_limit_bytes=63 * 1024 * 1024
        ),
        name="latent_attention",
    )(query_latent_rows, jnp.swapaxes(latent, 1, 2), wq_b, key_up_weight, value_up_weight, tau)


def solution(mesh):
    in_specs = (
        P("dp", "ctx", None),
        P("dp", "ctx", None),
        P("head", "ctx", None),
        P("head", "ctx", None),
        P("head", "ctx", None),
        P("head"),
    )
    out_specs = (P("dp", "ctx", "head"), P("head", "ctx", None), P("head", "ctx", None))
    return jax.shard_map(shards, mesh=mesh, in_specs=in_specs, out_specs=out_specs, check_vma=False)
```

```python
import functools

import jax
import jax.numpy as jnp
from jax import lax
from jax.experimental import pallas as pl
from jax.experimental.pallas import tpu as pltpu
from jax.sharding import PartitionSpec as P

MESH = pl.DeviceIdType.MESH
F32 = jnp.float32
BF16 = jnp.bfloat16
LOW = -1e30

HEADS = 6
HALF = 3
ROWS = 128
TOKS = 2 * ROWS
NOPE = 128
ROT = 64
LAT = 512
KEYW = LAT + ROT
RING = 8
CHIPS = 16
QUARTER = KEYW // 4
WROW = 48
UROW = 16
UPW = HALF * NOPE
WQW = UPW + 2 * 128
QROWS = HALF * TOKS
CHUNK = 2
WIDTH = CHUNK * TOKS
PLANE = 32


def kernel(
    x_ref, lat_ref, wq_ref, uk_ref, uv_ref, tau_ref,
    att_ref, nwq_ref, nuk_ref,
    wq, uk, uv, keys, xs, wq_in, uk_in, uv_in, wq_st, uk_st, uv_st, qf, table, score, mx, tot, acc, pk, pk2, att_out, att_in,
    ld_s, in_s, in_r, l1_s, l1_r, lx_s, wy_s, wy_r, wx_s, wx_r, z_s, z_r, ks_s, ks_r, pk_s, pk_r, fin_s, fin_r,
):
    dp = lax.axis_index("dp")
    ctx = lax.axis_index("ctx")
    z = lax.axis_index("head")
    core = lax.rem(ctx, 2)
    chip = ctx // 2
    xlo = chip // RING
    y = lax.rem(chip, RING)

    def wrap(v):
        return lax.rem(v + 2 * RING, RING)

    def dev(d, xl, yy, c, zz):
        return (d, (xl * RING + yy) * 2 + c, zz)

    sibling = dev(dp, xlo, y, 1 - core, z)
    y_next = (dev(dp, xlo, wrap(y + 1), core, z), dev(dp, xlo, wrap(y - 1), core, z))
    z_next = (dev(dp, xlo, y, core, wrap(z + 1)), dev(dp, xlo, y, core, wrap(z - 1)))
    def plane_dev(k):
        return dev(lax.rem(dp + k // 16, 2), lax.rem(xlo + (k // 8) % 2, 2), wrap(y + k % 8), core, z)

    def lay_out(c, wq_to, uk_to, uv_to):
        for i in range(HALF):
            h = HALF * c + i
            cols = slice(i * NOPE, (i + 1) * NOPE)
            wq_to[:, cols] = wq_in[h, :, :NOPE]
            uk_to[:, cols] = uk_in[h]
            uv_to[:, cols] = uv_in[h]
        rope = [wq_in[HALF * c + i, :, NOPE:] for i in range(HALF)]
        wq_to[:, UPW : UPW + 128] = jnp.concatenate(rope[:2], -1)
        wq_to[:, UPW + 128 :] = jnp.concatenate([rope[2], jnp.zeros((WROW, ROT), BF16)], -1)

    def wrows(c):
        return pl.ds(pl.multiple_of(c * WROW, WROW), WROW)

    def urows(c):
        return pl.ds(pl.multiple_of(c * UROW, UROW), UROW)


    def quarter(zz):
        return pl.ds(pl.multiple_of(lax.rem(zz + 8, 4) * QUARTER, QUARTER), QUARTER)

    loads = [
        pltpu.make_async_copy(wq_ref, wq_in, ld_s.at[0]),
        pltpu.make_async_copy(uk_ref, uk_in, ld_s.at[1]),
        pltpu.make_async_copy(uv_ref, uv_in, ld_s.at[2]),
        pltpu.make_async_copy(x_ref.at[0], xs.at[core], ld_s.at[3]),
        pltpu.make_async_copy(lat_ref.at[0], keys.at[chip, core], ld_s.at[4]),
    ]
    for load in loads:
        load.start()
    barrier = pltpu.get_barrier_semaphore()
    partners = [plane_dev(k) for d in (4, 3, 5, 2, 6, 1, 7, 0) for k in range(1, PLANE) if k % 8 == d]
    partners += [*z_next, sibling]
    for partner in partners:
        pl.semaphore_signal(barrier, inc=1, device_id=partner, device_id_type=MESH)
    for load in loads:
        load.wait()
    lay_out(1 - core, wq_st, uk_st, uv_st)
    lay_out(core, wq.at[chip, wrows(core)], uk.at[chip, urows(core)], uv.at[chip, urows(core)])
    pl.semaphore_wait(barrier, len(partners))

    sent = []

    def guarded(cond, f):
        if cond is None:
            f()
        else:
            pl.when(cond)(f)

    def send(make, cond=None):
        sent.append((cond, make))
        guarded(cond, lambda: make().start())

    def arrive(make, cond=None):
        guarded(cond, lambda: make().wait_recv())

    def copy(src, dst, ssem, rsem, to):
        return lambda: pltpu.make_async_remote_copy(
            src_ref=src(), dst_ref=dst(), send_sem=ssem, recv_sem=rsem, device_id=to, device_id_type=MESH
        )

    def in_copy(i, c):
        src, dst = (
            (lambda: wq_st, lambda: wq.at[chip, wrows(c)]),
            (lambda: uk_st, lambda: uk.at[chip, urows(c)]),
            (lambda: uv_st, lambda: uv.at[chip, urows(c)]),
            (lambda: xs.at[c], lambda: xs.at[c]),
        )[i]
        return copy(src, dst, in_s.at[i], in_r.at[i], sibling)

    ORDER = (0, -1, -2, -3, -4, 3, 2, 1)
    ACROSS = ((0, 0, 1, 1, 1, 1, 0, 1), (0, 1, 0, 1, 0, 1, 0, 1))

    def piece(a, xl, slot):
        p = xl * RING + wrap(y + ORDER[slot])
        if a < 6:
            src = core if a < 3 else 1 - core
            rows = pl.ds(pl.multiple_of(src * WROW + (a % 3) * 16, 16), 16)
            return lambda: wq.at[p, rows]
        return (lambda: uk.at[p]) if a == 6 else (lambda: uv.at[p])

    def wy_copy(a, way, s, slot):
        ref = piece(a, xlo, slot)
        return copy(ref, ref, wy_s.at[way, s - 1, a], wy_r.at[way, s - 1, a], y_next[way])

    def wx_copy(a, slot, xl, turn=0):
        ref = piece(a, xl, slot)
        down = jnp.where(xlo == 0, ACROSS[0][a], ACROSS[1][a])
        to = dev(lax.rem(dp + xlo + down, 2), 1 - xlo, wrap(y + turn), core, z)
        index = slot if turn == 0 else 4
        return copy(ref, ref, wx_s.at[index, a], wx_r.at[index, a], to)

    def w_begin(a):
        for way in (0, 1):
            send(wy_copy(a, way, 1, 0))
        send(wx_copy(a, 0, xlo))

    def w_step(s, parts=range(8)):
        for a in parts:
            for way in (0, 1):
                slot = s if way == 0 else 8 - s
                if s == 4 and a % 2 != way:
                    continue
                arrive(wy_copy(a, way, s, slot))
                if s < 3:
                    send(wy_copy(a, way, s + 1, slot))
                if s == 3 and a % 2 == way:
                    send(wx_copy(a, slot, xlo, 1 if way == 0 else -1))
                    send(wy_copy(a, way, s + 1, slot))
                if s < 4:
                    send(wx_copy(a, slot, xlo))

    def w_have(parts):
        for slot in range(8):
            for a in parts:
                arrive(wx_copy(a, slot, 1 - xlo))

    def keys_of(p, zz):
        return lambda: keys.at[p, core, quarter(zz), :]

    left = xlo == 0
    right = xlo == 1
    source = [chip] + [xlo * RING + wrap(y - k) for k in range(1, RING)] + list(range(RING))
    wanted = [None] + [y >= k for k in range(1, RING)] + [right] * RING

    def l1_copy(k):
        p = chip if k == 0 else source[k]
        return copy(keys_of(p, z), keys_of(p, z), l1_s.at[0], l1_r.at[k], plane_dev(8))

    def l1_begin():
        for k in (1, 7, 2, 6, 3, 5, 4):
            ref = keys_of(chip, z)
            send(
                copy(ref, ref, l1_s.at[k], l1_r.at[k], plane_dev(k)),
                jnp.logical_or(left, y + k < RING),
            )
        across(chip, left)

    def across(p, cond):
        ref = keys_of(p, z)
        i = 8 + lax.rem(p, RING)
        send(copy(ref, ref, lx_s.at[i - 8], l1_r.at[i], plane_dev(8)), cond)

    def l1_wait(k):
        arrive(l1_copy(k), jnp.logical_or(left, wanted[k]) if k < 8 else wanted[k])
        if k < 8:
            across(source[k], left)
        for way in (0, 1):
            send(z_copy(k, way, 1), wanted[k])

    def z_copy(k, way, s, src=None):
        sign = 1 if way == 0 else -1
        ref = keys_of(source[k], z - sign * (s - 1 if src is None else src))
        return copy(ref, ref, z_s.at[way, s - 1, k], z_r.at[way, s - 1, k], z_next[way])

    def z_turn(k):
        for way in (0, 1):
            arrive(z_copy(k, way, 1, 1), wanted[k])
        send(z_copy(k, k % 2, 2), wanted[k])

    def ks_copy(p, c):
        ref = lambda: keys.at[p, c]
        return lambda: copy(ref, ref, ks_s.at[p], ks_r.at[p], sibling)()

    def z_end(k):
        if k:
            arrive(z_copy(k, k % 2, 2, 2), wanted[k])
        send(ks_copy(source[k], core), wanted[k])

    def chip_wait(p):
        arrive(ks_copy(p, 1 - core), p <= chip)

    half = ROT // 2

    def first_half():
        return lax.rem(lax.broadcasted_iota(jnp.int32, (TOKS, 128), 1), ROT) < half

    def prepare():
        lane = lax.broadcasted_iota(jnp.int32, (TOKS, 128), 1)
        row = lax.broadcasted_iota(jnp.int32, (TOKS, 128), 0)
        expo = (-2.0 / ROT) * lax.rem(lane, half).astype(F32)
        freq = jnp.exp(expo * jnp.log(F32(50000.0)))
        angle = (chip * TOKS + row).astype(F32) * freq
        sine = jnp.sin(angle)
        table[0] = jnp.cos(angle)
        table[1] = jnp.where(first_half(), -sine, sine)
        mx[...] = jnp.full_like(mx, LOW)
        tot[...] = jnp.zeros_like(tot)
        acc[...] = jnp.zeros_like(acc)

    def project():
        xx = xs[...].reshape(TOKS, 2 * CHIPS * WROW)
        w = wq[...].reshape(2 * CHIPS * WROW, WQW)
        query = jnp.dot(xx, w, preferred_element_type=F32)
        first = first_half()
        cosine = table[0]
        sine = table[1]
        scale = F32((NOPE + ROT) ** -0.5)
        ukw = uk[...].reshape(LAT, UPW)
        rots = []
        for j in range(2):
            q = query[:, UPW + j * 128 : UPW + (j + 1) * 128]
            other = jnp.where(first, pltpu.roll(q, 128 - half, 1), pltpu.roll(q, half, 1))
            rots.append((q * cosine + other * sine) * scale)
        rots = [rots[0][:, :ROT], pltpu.roll(rots[0], ROT, 1)[:, :ROT], rots[1][:, :ROT]]
        for i in range(HALF):
            rows = pl.ds(i * TOKS, TOKS)
            nope = query[:, i * NOPE : (i + 1) * NOPE].astype(BF16)
            q_lat = lax.dot_general(
                nope, ukw[:, i * NOPE : (i + 1) * NOPE], (((1,), (1,)), ((), ())), preferred_element_type=F32
            )
            qf[rows, :LAT] = (q_lat * scale).astype(BF16)
            qf[rows, LAT:] = rots[i].astype(BF16)

    def keys_at(j):
        at = [jnp.minimum(CHUNK * j + a, chip) for a in range(CHUNK)]
        return jnp.concatenate([keys[p, c] for p in at for c in range(2)], -1)

    def scores(j, masked):
        kt = keys_at(j)
        for i in range(HALF):
            rows = pl.ds(i * TOKS, TOKS)
            s = jnp.dot(qf[rows, :], kt, preferred_element_type=F32)
            if masked:
                t = (chip - CHUNK * j) * TOKS + lax.broadcasted_iota(jnp.int32, (TOKS, WIDTH), 0)
                s = jnp.where(lax.broadcasted_iota(jnp.int32, (TOKS, WIDTH), 1) <= t, s, LOW)
            score[j, rows, :] = s
            parts = [s[:, b * 128 : (b + 1) * 128] for b in range(WIDTH // 128)]
            mx[rows, :] = functools.reduce(jnp.maximum, parts, mx[rows, :])

    def scores_all(events):
        steps = CHIPS // CHUNK

        def body(i, _):
            for at, slots in events.items():
                @pl.when(i == at)
                def _():
                    for k in slots:
                        z_end(k)

            j = lax.rem(i + xlo * (steps // 2), steps)
            for a in range(CHUNK):
                chip_wait(CHUNK * j + a)

            @pl.when(j < chip // CHUNK)
            def _():
                scores(j, False)

            @pl.when(j == chip // CHUNK)
            def _():
                scores(j, True)

            return 0

        lax.fori_loop(0, steps, body, 0)

    def mix_all():
        mx[...] = jnp.broadcast_to(jnp.max(mx[...], -1, keepdims=True), mx.shape)

        def body(j, _):
            kt = keys_at(j)[:LAT]
            for i in range(HALF):
                rows = pl.ds(i * TOKS, TOKS)
                top = mx[rows, :]
                parts = [jnp.exp(score[j, rows, b * 128 : (b + 1) * 128] - top) for b in range(WIDTH // 128)]
                tot[rows, :] += functools.reduce(jnp.add, parts)
                prob = jnp.concatenate([p.astype(BF16) for p in parts], -1)
                acc[rows, :] += lax.dot_general(prob, kt, (((1,), (1,)), ((), ())), preferred_element_type=F32)
            return 0

        lax.fori_loop(0, chip // CHUNK + 1, body, 0)

    def peak_copy(k):
        return copy(lambda: pk.at[0], lambda: pk.at[k], pk_s.at[k], pk_r.at[k], plane_dev(k))

    def peak_begin():
        for i in range(HALF):
            pk[0, i : i + 1, :] = jnp.max(mx[pl.ds(i * TOKS, TOKS), :], 0, keepdims=True)
        pk[0, HALF:, :] = jnp.full((8 - HALF, 128), LOW, F32)
        for k in [k for d in (4, 3, 5, 2, 6, 1, 7, 0) for k in range(1, PLANE) if k % 8 == d]:
            send(peak_copy(k))

    def fin_copy(i, c):
        src, dst = (
            (lambda: pk2.at[c], lambda: pk2.at[c]),
            (lambda: att_out, lambda: att_in),
        )[i]
        return copy(src, dst, fin_s.at[i], fin_r.at[i], sibling)

    def peak_end():
        for k in range(1, PLANE):
            arrive(peak_copy(k))
        pk2[core] = jnp.max(pk[...], 0)
        send(fin_copy(0, core))

    def finish():
        arrive(fin_copy(0, 1 - core))
        for h in range(HEADS):
            peak = jnp.max(pk2[h // HALF, h % HALF : h % HALF + 1, :], -1, keepdims=True)
            limit = jnp.full((1, 128), tau_ref[h].astype(F32), F32)
            gamma = limit / jnp.maximum(peak, limit)
            root = jnp.sqrt(gamma)
            nwq_ref[h, :, :NOPE] = (wq_in[h, :, :NOPE].astype(F32) * root).astype(BF16)
            nwq_ref[h, :, NOPE:] = (wq_in[h, :, NOPE:].astype(F32) * gamma[:, :ROT]).astype(BF16)
            nuk_ref[h] = (uk_in[h].astype(F32) * root).astype(BF16)

    def output():
        uvw = uv[...].reshape(LAT, UPW)

        def of(c, i):
            rows = pl.ds(pl.multiple_of(i * TOKS + c * ROWS, ROWS), ROWS)
            total = jnp.sum(tot[rows, :], -1, keepdims=True)
            mixed = (acc[rows, :] / total).astype(BF16)
            w = uvw[:, i * NOPE : (i + 1) * NOPE]
            return jnp.dot(mixed, w, preferred_element_type=F32).astype(BF16)

        for i in range(HALF):
            att_out[:, i * NOPE : (i + 1) * NOPE] = of(1 - core, i)
        send(fin_copy(1, core))
        for i in range(HALF):
            att_ref[0, :, pl.ds(pl.multiple_of((core * HALF + i) * NOPE, NOPE), NOPE)] = of(core, i)

    def output_end():
        arrive(fin_copy(1, 1 - core))
        att_ref[0, :, pl.ds(pl.multiple_of((1 - core) * UPW, UPW), UPW)] = att_in[...]

    for i in range(4):
        send(in_copy(i, core))
    l1_begin()
    for a in range(3):
        w_begin(a)
    arrive(in_copy(0, 1 - core))
    for a in (3, 4, 5):
        w_begin(a)
    arrive(in_copy(1, 1 - core))
    w_begin(6)
    arrive(in_copy(2, 1 - core))
    w_begin(7)
    z_end(0)
    prepare()
    for k in (1, 7, 2, 6, 3, 5, 4):
        l1_wait(k)
    w_step(1, range(8))
    for k in range(8, 16):
        l1_wait(k)
    w_step(2, range(8))
    for k in (1, 7, 2, 6, 3, 5, 4):
        z_turn(k)
    w_step(3, range(8))
    for k in range(8, 16):
        z_turn(k)
    for k in (1, 7, 2, 6, 3, 5, 4):
        z_end(k)
    arrive(in_copy(3, 1 - core))
    w_step(4, range(8))
    w_have(range(7))
    project()
    scores_all({1: (8, 9, 10, 11), 3: (12, 13, 14, 15)})
    peak_begin()
    mix_all()
    w_have((7,))
    output()
    peak_end()
    output_end()
    finish()
    for cond, make in sent:
        guarded(cond, lambda: make().wait_send())


def hand_over(a_ref, b_ref, c_ref, a_out, b_out, c_out):
    a_out[...] = a_ref[...]
    b_out[...] = b_ref[...]
    c_out[...] = c_ref[...]


def shards(query_latent_rows, latent, wq_b, key_up_weight, value_up_weight, tau):
    dma = pltpu.SemaphoreType.DMA
    shapes = (
        jax.ShapeDtypeStruct((1, ROWS, HEADS * NOPE), BF16),
        jax.ShapeDtypeStruct(wq_b.shape, BF16),
        jax.ShapeDtypeStruct(key_up_weight.shape, BF16),
    )
    vmem = pl.BlockSpec(memory_space=pltpu.VMEM)
    hbm = pl.BlockSpec(memory_space=pltpu.HBM)
    made = pl.pallas_call(
        kernel,
        out_shape=shapes,
        in_specs=[hbm] * 5 + [pl.BlockSpec(memory_space=pltpu.SMEM)],
        out_specs=(vmem,) * 3,
        scratch_shapes=[
            pltpu.VMEM((CHIPS, 2 * WROW, WQW), BF16),
            pltpu.VMEM((CHIPS, 2 * UROW, UPW), BF16),
            pltpu.VMEM((CHIPS, 2 * UROW, UPW), BF16),
            pltpu.VMEM((CHIPS, 2, KEYW, ROWS), BF16),
            pltpu.VMEM((2, ROWS, 2 * CHIPS * WROW), BF16),
            pltpu.VMEM((HEADS, WROW, NOPE + ROT), BF16),
            pltpu.VMEM((HEADS, UROW, NOPE), BF16),
            pltpu.VMEM((HEADS, UROW, NOPE), BF16),
            pltpu.VMEM((WROW, WQW), BF16),
            pltpu.VMEM((UROW, UPW), BF16),
            pltpu.VMEM((UROW, UPW), BF16),
            pltpu.VMEM((QROWS, KEYW), BF16),
            pltpu.VMEM((2, TOKS, 128), F32),
            pltpu.VMEM((CHIPS // CHUNK, QROWS, WIDTH), F32),
            pltpu.VMEM((QROWS, 128), F32),
            pltpu.VMEM((QROWS, 128), F32),
            pltpu.VMEM((QROWS, LAT), F32),
            pltpu.VMEM((PLANE, 8, 128), F32),
            pltpu.VMEM((2, 8, 128), F32),
            pltpu.VMEM((ROWS, UPW), BF16),
            pltpu.VMEM((ROWS, UPW), BF16),
            dma((5,)),
            dma((4,)), dma((4,)),
            dma((8,)), dma((16,)),
            dma((8,)),
            dma((2, 4, 8)), dma((2, 4, 8)),
            dma((8, 8)), dma((8, 8)),
            dma((2, 2, CHIPS)), dma((2, 2, CHIPS)),
            dma((CHIPS,)), dma((CHIPS,)),
            dma((PLANE,)), dma((PLANE,)),
            dma((2,)), dma((2,)),
        ],
        compiler_params=pltpu.CompilerParams(
            collective_id=0, has_side_effects=True, vmem_limit_bytes=63 * 1024 * 1024
        ),
        name="latent_attention",
    )(query_latent_rows, jnp.swapaxes(latent, 1, 2), wq_b, key_up_weight, value_up_weight, tau)
    return pl.pallas_call(
        hand_over,
        out_shape=shapes,
        in_specs=[vmem] * 3,
        out_specs=(vmem,) * 3,
        name="hand_over",
    )(*made)


def solution(mesh):
    in_specs = (
        P("dp", "ctx", None),
        P("dp", "ctx", None),
        P("head", "ctx", None),
        P("head", "ctx", None),
        P("head", "ctx", None),
        P("head"),
    )
    out_specs = (P("dp", "ctx", "head"), P("head", "ctx", None), P("head", "ctx", None))
    return jax.shard_map(shards, mesh=mesh, in_specs=in_specs, out_specs=out_specs, check_vma=False)
```

```python
import functools

import jax
import jax.numpy as jnp
from jax import lax
from jax.experimental import pallas as pl
from jax.experimental.pallas import tpu as pltpu
from jax.sharding import PartitionSpec as P

MESH = pl.DeviceIdType.MESH
F32 = jnp.float32
BF16 = jnp.bfloat16
LOW = -1e30

HEADS = 6
HALF = 3
ROWS = 128
TOKS = 2 * ROWS
NOPE = 128
ROT = 64
LAT = 512
KEYW = LAT + ROT
RING = 8
CHIPS = 16
QUARTER = KEYW // 4
WROW = 48
UROW = 16
UPW = HALF * NOPE
WQW = UPW + 2 * 128
QROWS = HALF * TOKS
CHUNK = 2
WIDTH = CHUNK * TOKS
PLANE = 32


def kernel(
    x_ref, lat_ref, wq_ref, uk_ref, uv_ref, tau_ref,
    att_ref, nwq_ref, nuk_ref,
    wq, uk, uv, keys, xs, wq_in, uk_in, uv_in, wq_st, uk_st, uv_st, qf, table, score, mx, tot, acc, pk, pk2, att_out, att_in,
    ld_s, in_s, in_r, l1_s, l1_r, lx_s, wy_s, wy_r, wx_s, wx_r, z_s, z_r, ks_s, ks_r, pk_s, pk_r, fin_s, fin_r,
):
    dp = lax.axis_index("dp")
    ctx = lax.axis_index("ctx")
    z = lax.axis_index("head")
    core = lax.rem(ctx, 2)
    chip = ctx // 2
    xlo = chip // RING
    y = lax.rem(chip, RING)

    def wrap(v):
        return lax.rem(v + 2 * RING, RING)

    def dev(d, xl, yy, c, zz):
        return (d, (xl * RING + yy) * 2 + c, zz)

    sibling = dev(dp, xlo, y, 1 - core, z)
    y_next = (dev(dp, xlo, wrap(y + 1), core, z), dev(dp, xlo, wrap(y - 1), core, z))
    z_next = (dev(dp, xlo, y, core, wrap(z + 1)), dev(dp, xlo, y, core, wrap(z - 1)))
    def plane_dev(k):
        return dev(lax.rem(dp + k // 16, 2), lax.rem(xlo + (k // 8) % 2, 2), wrap(y + k % 8), core, z)

    def lay_out(c, wq_to, uk_to, uv_to):
        for i in range(HALF):
            h = HALF * c + i
            cols = slice(i * NOPE, (i + 1) * NOPE)
            wq_to[:, cols] = wq_in[h, :, :NOPE]
            uk_to[:, cols] = uk_in[h]
            uv_to[:, cols] = uv_in[h]
        rope = [wq_in[HALF * c + i, :, NOPE:] for i in range(HALF)]
        wq_to[:, UPW : UPW + 128] = jnp.concatenate(rope[:2], -1)
        wq_to[:, UPW + 128 :] = jnp.concatenate([rope[2], jnp.zeros((WROW, ROT), BF16)], -1)

    def wrows(c):
        return pl.ds(pl.multiple_of(c * WROW, WROW), WROW)

    def urows(c):
        return pl.ds(pl.multiple_of(c * UROW, UROW), UROW)


    def quarter(zz):
        return pl.ds(pl.multiple_of(lax.rem(zz + 8, 4) * QUARTER, QUARTER), QUARTER)

    loads = [
        pltpu.make_async_copy(wq_ref, wq_in, ld_s.at[0]),
        pltpu.make_async_copy(uk_ref, uk_in, ld_s.at[1]),
        pltpu.make_async_copy(uv_ref, uv_in, ld_s.at[2]),
        pltpu.make_async_copy(x_ref.at[0], xs.at[core], ld_s.at[3]),
        pltpu.make_async_copy(lat_ref.at[0], keys.at[chip, core], ld_s.at[4]),
    ]
    for load in loads:
        load.start()
    barrier = pltpu.get_barrier_semaphore()
    partners = [plane_dev(k) for d in (4, 3, 5, 2, 6, 1, 7, 0) for k in range(1, PLANE) if k % 8 == d]
    partners += [*z_next, sibling]
    for partner in partners:
        pl.semaphore_signal(barrier, inc=1, device_id=partner, device_id_type=MESH)
    for load in loads:
        load.wait()
    lay_out(1 - core, wq_st, uk_st, uv_st)
    lay_out(core, wq.at[chip, wrows(core)], uk.at[chip, urows(core)], uv.at[chip, urows(core)])
    pl.semaphore_wait(barrier, len(partners))

    sent = []

    def guarded(cond, f):
        if cond is None:
            f()
        else:
            pl.when(cond)(f)

    def send(make, cond=None):
        sent.append((cond, make))
        guarded(cond, lambda: make().start())

    def drain(upto):
        for cond, make in sent[:upto]:
            guarded(cond, lambda: make().wait_send())
        del sent[:upto]

    def arrive(make, cond=None):
        guarded(cond, lambda: make().wait_recv())

    def copy(src, dst, ssem, rsem, to):
        return lambda: pltpu.make_async_remote_copy(
            src_ref=src(), dst_ref=dst(), send_sem=ssem, recv_sem=rsem, device_id=to, device_id_type=MESH
        )

    def in_copy(i, c):
        src, dst = (
            (lambda: wq_st, lambda: wq.at[chip, wrows(c)]),
            (lambda: uk_st, lambda: uk.at[chip, urows(c)]),
            (lambda: uv_st, lambda: uv.at[chip, urows(c)]),
            (lambda: xs.at[c], lambda: xs.at[c]),
        )[i]
        return copy(src, dst, in_s.at[i], in_r.at[i], sibling)

    ORDER = (0, -1, -2, -3, -4, 3, 2, 1)
    ACROSS = ((0, 0, 1, 1, 1, 1, 0, 1), (0, 1, 0, 1, 0, 1, 0, 1))

    def piece(a, xl, slot):
        p = xl * RING + wrap(y + ORDER[slot])
        if a < 6:
            src = core if a < 3 else 1 - core
            rows = pl.ds(pl.multiple_of(src * WROW + (a % 3) * 16, 16), 16)
            return lambda: wq.at[p, rows]
        return (lambda: uk.at[p]) if a == 6 else (lambda: uv.at[p])

    def wy_copy(a, way, s, slot):
        ref = piece(a, xlo, slot)
        return copy(ref, ref, wy_s.at[way, s - 1, a], wy_r.at[way, s - 1, a], y_next[way])

    def wx_copy(a, slot, xl, turn=0):
        ref = piece(a, xl, slot)
        down = jnp.where(xlo == 0, ACROSS[0][a], ACROSS[1][a])
        to = dev(lax.rem(dp + xlo + down, 2), 1 - xlo, wrap(y + turn), core, z)
        index = slot if turn == 0 else 4
        return copy(ref, ref, wx_s.at[index, a], wx_r.at[index, a], to)

    def w_begin(a):
        for way in (0, 1):
            send(wy_copy(a, way, 1, 0))
        send(wx_copy(a, 0, xlo))

    def w_step(s, parts=range(8)):
        for a in parts:
            for way in (0, 1):
                slot = s if way == 0 else 8 - s
                if s == 4 and a % 2 != way:
                    continue
                arrive(wy_copy(a, way, s, slot))
                if s < 3:
                    send(wy_copy(a, way, s + 1, slot))
                if s == 3 and a % 2 == way:
                    send(wx_copy(a, slot, xlo, 1 if way == 0 else -1))
                    send(wy_copy(a, way, s + 1, slot))
                if s < 4:
                    send(wx_copy(a, slot, xlo))

    def w_have(parts):
        for slot in range(8):
            for a in parts:
                arrive(wx_copy(a, slot, 1 - xlo))

    def keys_of(p, zz):
        return lambda: keys.at[p, core, quarter(zz), :]

    left = xlo == 0
    right = xlo == 1
    source = [chip] + [xlo * RING + wrap(y - k) for k in range(1, RING)] + list(range(RING))
    wanted = [None] + [y >= k for k in range(1, RING)] + [right] * RING

    def l1_copy(k):
        p = chip if k == 0 else source[k]
        return copy(keys_of(p, z), keys_of(p, z), l1_s.at[0], l1_r.at[k], plane_dev(8))

    def l1_begin():
        for k in (1, 7, 2, 6, 3, 5, 4):
            ref = keys_of(chip, z)
            send(
                copy(ref, ref, l1_s.at[k], l1_r.at[k], plane_dev(k)),
                jnp.logical_or(left, y + k < RING),
            )
        across(chip, left)

    def across(p, cond):
        ref = keys_of(p, z)
        i = 8 + lax.rem(p, RING)
        send(copy(ref, ref, lx_s.at[i - 8], l1_r.at[i], plane_dev(8)), cond)

    def l1_wait(k):
        arrive(l1_copy(k), jnp.logical_or(left, wanted[k]) if k < 8 else wanted[k])
        if k < 8:
            across(source[k], left)
        for way in (0, 1):
            send(z_copy(k, way, 1), wanted[k])

    def z_copy(k, way, s, src=None):
        sign = 1 if way == 0 else -1
        ref = keys_of(source[k], z - sign * (s - 1 if src is None else src))
        return copy(ref, ref, z_s.at[way, s - 1, k], z_r.at[way, s - 1, k], z_next[way])

    def z_turn(k):
        for way in (0, 1):
            arrive(z_copy(k, way, 1, 1), wanted[k])
        send(z_copy(k, k % 2, 2), wanted[k])

    def ks_copy(p, c):
        ref = lambda: keys.at[p, c]
        return lambda: copy(ref, ref, ks_s.at[p], ks_r.at[p], sibling)()

    def z_end(k):
        if k:
            arrive(z_copy(k, k % 2, 2, 2), wanted[k])
        send(ks_copy(source[k], core), wanted[k])

    def chip_wait(p):
        arrive(ks_copy(p, 1 - core), p <= chip)

    half = ROT // 2

    def first_half():
        return lax.rem(lax.broadcasted_iota(jnp.int32, (TOKS, 128), 1), ROT) < half

    def prepare():
        lane = lax.broadcasted_iota(jnp.int32, (TOKS, 128), 1)
        row = lax.broadcasted_iota(jnp.int32, (TOKS, 128), 0)
        expo = (-2.0 / ROT) * lax.rem(lane, half).astype(F32)
        freq = jnp.exp(expo * jnp.log(F32(50000.0)))
        angle = (chip * TOKS + row).astype(F32) * freq
        sine = jnp.sin(angle)
        table[0] = jnp.cos(angle)
        table[1] = jnp.where(first_half(), -sine, sine)
        mx[...] = jnp.full_like(mx, LOW)
        tot[...] = jnp.zeros_like(tot)
        acc[...] = jnp.zeros_like(acc)

    def project():
        xx = xs[...].reshape(TOKS, 2 * CHIPS * WROW)
        w = wq[...].reshape(2 * CHIPS * WROW, WQW)
        query = jnp.dot(xx, w, preferred_element_type=F32)
        first = first_half()
        cosine = table[0]
        sine = table[1]
        scale = F32((NOPE + ROT) ** -0.5)
        ukw = uk[...].reshape(LAT, UPW)
        rots = []
        for j in range(2):
            q = query[:, UPW + j * 128 : UPW + (j + 1) * 128]
            other = jnp.where(first, pltpu.roll(q, 128 - half, 1), pltpu.roll(q, half, 1))
            rots.append((q * cosine + other * sine) * scale)
        rots = [rots[0][:, :ROT], pltpu.roll(rots[0], ROT, 1)[:, :ROT], rots[1][:, :ROT]]
        for i in range(HALF):
            rows = pl.ds(i * TOKS, TOKS)
            nope = query[:, i * NOPE : (i + 1) * NOPE].astype(BF16)
            q_lat = lax.dot_general(
                nope, ukw[:, i * NOPE : (i + 1) * NOPE], (((1,), (1,)), ((), ())), preferred_element_type=F32
            )
            qf[rows, :LAT] = (q_lat * scale).astype(BF16)
            qf[rows, LAT:] = rots[i].astype(BF16)

    def keys_at(j):
        at = [jnp.minimum(CHUNK * j + a, chip) for a in range(CHUNK)]
        return jnp.concatenate([keys[p, c] for p in at for c in range(2)], -1)

    def scores(j, masked):
        kt = keys_at(j)
        for i in range(HALF):
            rows = pl.ds(i * TOKS, TOKS)
            s = jnp.dot(qf[rows, :], kt, preferred_element_type=F32)
            if masked:
                t = (chip - CHUNK * j) * TOKS + lax.broadcasted_iota(jnp.int32, (TOKS, WIDTH), 0)
                s = jnp.where(lax.broadcasted_iota(jnp.int32, (TOKS, WIDTH), 1) <= t, s, LOW)
            score[j, rows, :] = s
            parts = [s[:, b * 128 : (b + 1) * 128] for b in range(WIDTH // 128)]
            mx[rows, :] = functools.reduce(jnp.maximum, parts, mx[rows, :])

    def scores_all(events):
        steps = CHIPS // CHUNK

        def body(i, _):
            for at, slots in events.items():
                @pl.when(i == at)
                def _():
                    for k in slots:
                        z_end(k)

            j = lax.rem(i + xlo * (steps // 2), steps)
            for a in range(CHUNK):
                chip_wait(CHUNK * j + a)

            @pl.when(j < chip // CHUNK)
            def _():
                scores(j, False)

            @pl.when(j == chip // CHUNK)
            def _():
                scores(j, True)

            return 0

        lax.fori_loop(0, steps, body, 0)

    def mix_all():
        mx[...] = jnp.broadcast_to(jnp.max(mx[...], -1, keepdims=True), mx.shape)

        def body(j, _):
            kt = keys_at(j)[:LAT]
            for i in range(HALF):
                rows = pl.ds(i * TOKS, TOKS)
                top = mx[rows, :]
                parts = [jnp.exp(score[j, rows, b * 128 : (b + 1) * 128] - top) for b in range(WIDTH // 128)]
                tot[rows, :] += functools.reduce(jnp.add, parts)
                prob = jnp.concatenate([p.astype(BF16) for p in parts], -1)
                acc[rows, :] += lax.dot_general(prob, kt, (((1,), (1,)), ((), ())), preferred_element_type=F32)
            return 0

        lax.fori_loop(0, chip // CHUNK + 1, body, 0)

    def peak_copy(k):
        return copy(lambda: pk.at[0], lambda: pk.at[k], pk_s.at[k], pk_r.at[k], plane_dev(k))

    def peak_begin():
        for i in range(HALF):
            pk[0, i : i + 1, :] = jnp.max(mx[pl.ds(i * TOKS, TOKS), :], 0, keepdims=True)
        pk[0, HALF:, :] = jnp.full((8 - HALF, 128), LOW, F32)
        for k in [k for d in (4, 3, 5, 2, 6, 1, 7, 0) for k in range(1, PLANE) if k % 8 == d]:
            send(peak_copy(k))

    def fin_copy(i, c):
        src, dst = (
            (lambda: pk2.at[c], lambda: pk2.at[c]),
            (lambda: att_out, lambda: att_in),
        )[i]
        return copy(src, dst, fin_s.at[i], fin_r.at[i], sibling)

    def peak_end():
        for k in range(1, PLANE):
            arrive(peak_copy(k))
        pk2[core] = jnp.max(pk[...], 0)
        send(fin_copy(0, core))

    def finish():
        arrive(fin_copy(0, 1 - core))
        for h in range(HEADS):
            peak = jnp.max(pk2[h // HALF, h % HALF : h % HALF + 1, :], -1, keepdims=True)
            limit = jnp.full((1, 128), tau_ref[h].astype(F32), F32)
            gamma = limit / jnp.maximum(peak, limit)
            root = jnp.sqrt(gamma)
            nwq_ref[h, :, :NOPE] = (wq_in[h, :, :NOPE].astype(F32) * root).astype(BF16)
            nwq_ref[h, :, NOPE:] = (wq_in[h, :, NOPE:].astype(F32) * gamma[:, :ROT]).astype(BF16)
            nuk_ref[h] = (uk_in[h].astype(F32) * root).astype(BF16)

    def output():
        uvw = uv[...].reshape(LAT, UPW)

        def of(c, i):
            rows = pl.ds(pl.multiple_of(i * TOKS + c * ROWS, ROWS), ROWS)
            total = jnp.sum(tot[rows, :], -1, keepdims=True)
            mixed = (acc[rows, :] / total).astype(BF16)
            w = uvw[:, i * NOPE : (i + 1) * NOPE]
            return jnp.dot(mixed, w, preferred_element_type=F32).astype(BF16)

        for i in range(HALF):
            att_out[:, i * NOPE : (i + 1) * NOPE] = of(1 - core, i)
        send(fin_copy(1, core))
        for i in range(HALF):
            att_ref[0, :, pl.ds(pl.multiple_of((core * HALF + i) * NOPE, NOPE), NOPE)] = of(core, i)

    def output_end():
        arrive(fin_copy(1, 1 - core))
        att_ref[0, :, pl.ds(pl.multiple_of((1 - core) * UPW, UPW), UPW)] = att_in[...]

    for i in range(4):
        send(in_copy(i, core))
    l1_begin()
    for a in range(3):
        w_begin(a)
    arrive(in_copy(0, 1 - core))
    for a in (3, 4, 5):
        w_begin(a)
    arrive(in_copy(1, 1 - core))
    w_begin(6)
    arrive(in_copy(2, 1 - core))
    w_begin(7)
    z_end(0)
    prepare()
    for k in (1, 7, 2, 6, 3, 5, 4):
        l1_wait(k)
    w_step(1, range(8))
    for a in range(8):
        l1_wait(8 + a)
        w_step(2, (a,))
    early = len(sent)
    for k in (1, 7, 2, 6, 3, 5, 4):
        z_turn(k)
    w_step(3, range(8))
    for k in range(8, 16):
        z_turn(k)
    for k in (1, 7, 2, 6, 3, 5, 4):
        z_end(k)
    arrive(in_copy(3, 1 - core))
    w_step(4, range(8))
    drain(early)
    w_have(range(7))
    project()
    scores_all({1: (8, 9, 10, 11), 3: (12, 13, 14, 15)})
    peak_begin()
    mix_all()
    w_have((7,))
    output()
    drain(len(sent) - 1)
    peak_end()
    output_end()
    finish()
    drain(len(sent))


def hand_over(a_ref, b_ref, c_ref, a_out, b_out, c_out):
    a_out[...] = a_ref[...]
    b_out[...] = b_ref[...]
    c_out[...] = c_ref[...]


def shards(query_latent_rows, latent, wq_b, key_up_weight, value_up_weight, tau):
    dma = pltpu.SemaphoreType.DMA
    shapes = (
        jax.ShapeDtypeStruct((1, ROWS, HEADS * NOPE), BF16),
        jax.ShapeDtypeStruct(wq_b.shape, BF16),
        jax.ShapeDtypeStruct(key_up_weight.shape, BF16),
    )
    vmem = pl.BlockSpec(memory_space=pltpu.VMEM)
    hbm = pl.BlockSpec(memory_space=pltpu.HBM)
    made = pl.pallas_call(
        kernel,
        out_shape=shapes,
        in_specs=[hbm] * 5 + [pl.BlockSpec(memory_space=pltpu.SMEM)],
        out_specs=(vmem,) * 3,
        scratch_shapes=[
            pltpu.VMEM((CHIPS, 2 * WROW, WQW), BF16),
            pltpu.VMEM((CHIPS, 2 * UROW, UPW), BF16),
            pltpu.VMEM((CHIPS, 2 * UROW, UPW), BF16),
            pltpu.VMEM((CHIPS, 2, KEYW, ROWS), BF16),
            pltpu.VMEM((2, ROWS, 2 * CHIPS * WROW), BF16),
            pltpu.VMEM((HEADS, WROW, NOPE + ROT), BF16),
            pltpu.VMEM((HEADS, UROW, NOPE), BF16),
            pltpu.VMEM((HEADS, UROW, NOPE), BF16),
            pltpu.VMEM((WROW, WQW), BF16),
            pltpu.VMEM((UROW, UPW), BF16),
            pltpu.VMEM((UROW, UPW), BF16),
            pltpu.VMEM((QROWS, KEYW), BF16),
            pltpu.VMEM((2, TOKS, 128), F32),
            pltpu.VMEM((CHIPS // CHUNK, QROWS, WIDTH), F32),
            pltpu.VMEM((QROWS, 128), F32),
            pltpu.VMEM((QROWS, 128), F32),
            pltpu.VMEM((QROWS, LAT), F32),
            pltpu.VMEM((PLANE, 8, 128), F32),
            pltpu.VMEM((2, 8, 128), F32),
            pltpu.VMEM((ROWS, UPW), BF16),
            pltpu.VMEM((ROWS, UPW), BF16),
            dma((5,)),
            dma((4,)), dma((4,)),
            dma((8,)), dma((16,)),
            dma((8,)),
            dma((2, 4, 8)), dma((2, 4, 8)),
            dma((8, 8)), dma((8, 8)),
            dma((2, 2, CHIPS)), dma((2, 2, CHIPS)),
            dma((CHIPS,)), dma((CHIPS,)),
            dma((PLANE,)), dma((PLANE,)),
            dma((2,)), dma((2,)),
        ],
        compiler_params=pltpu.CompilerParams(
            collective_id=0, has_side_effects=True, vmem_limit_bytes=63 * 1024 * 1024
        ),
        name="latent_attention",
    )(query_latent_rows, jnp.swapaxes(latent, 1, 2), wq_b, key_up_weight, value_up_weight, tau)
    return pl.pallas_call(
        hand_over,
        out_shape=shapes,
        in_specs=[vmem] * 3,
        out_specs=(vmem,) * 3,
        name="hand_over",
    )(*made)


def solution(mesh):
    in_specs = (
        P("dp", "ctx", None),
        P("dp", "ctx", None),
        P("head", "ctx", None),
        P("head", "ctx", None),
        P("head", "ctx", None),
        P("head"),
    )
    out_specs = (P("dp", "ctx", "head"), P("head", "ctx", None), P("head", "ctx", None))
    return jax.shard_map(shards, mesh=mesh, in_specs=in_specs, out_specs=out_specs, check_vma=False)
```
